32 devices in a mesh: dp: 8 (over z, x), mp: 4 (over y, core).
Axes of the slice: x: 2, y: 2, z: 4, core: 2. Of those that a mesh axis runs over, the one named last changes fastest.
Arguments:
- hidden: bfloat16 [1024, 12288], P('dp', 'mp'), may hold values from -6 to 6
- w_out: bfloat16 [6144, 12288], P('dp', 'mp'), may hold values from -0.0546875 to 0.0546875
- direction: bfloat16 [6144, 12288], P('dp', 'mp'), may hold values from -6 to 6
- targets: bfloat16 [1024, 6144], P('mp', 'dp'), may hold values from -6 to 6
- codes: int32 [4], replicated, may hold values from 0 to 3
- code_weights: float32 [4], replicated, may hold values from 0.5 to 2
Outputs:
- inverse_product: float32 [6144, 12288], P('dp', 'mp')
The draws below stay inside these ranges and needn't reach their ends.
All inputs are finite; a program needn't handle non-finite values.
Results may differ from the reference program's by a relative error of at most 0.006.
Values may be sent and summed in bfloat16 or wider, within the bound.
No kernel may reach another device: no remote copies, remote signals or barrier semaphores. Data moves between devices by JAX's collectives and lax.ppermute only.
A program may use at most 128 MiB of HBM per device.

```python
import math
import jax
import jax.numpy as jnp
from jax import lax

D = 6144
FF = 12288
GRID = 16
CODES = 4
PATCHES = 256
TOKENS = 1024
IMAGES = 4
N_MP = 4


def with_ends(values, stream_key, smallest, largest):
    index_at = [jax.random.randint(jax.random.fold_in(stream_key, axis), (), 0, length) for axis, length in enumerate(values.shape)]
    widest = values.shape.index(max(values.shape))
    neighbour = index_at[:widest] + [(index_at[widest] + 1) % values.shape[widest]] + index_at[widest + 1:]
    return values.at[tuple(index_at)].set(smallest).at[tuple(neighbour)].set(largest)


def shard_levels(own_key, shape, cuts, least, top_value):
    loudness, own = 1.0, jax.random.fold_in(own_key, 6)
    for axis_at, parts in cuts:
        heights = jnp.exp(jax.random.uniform(jax.random.fold_in(own, axis_at), (parts,), jnp.float32, least / len(cuts), top_value / len(cuts)))
        loudness = loudness * jnp.repeat(heights, shape[axis_at] // parts).reshape([-1 if axis == axis_at else 1 for axis in range(len(shape))])
    return loudness


def scatter_about(key, shape, deviation, reach, split=(), held_as=jnp.bfloat16):
    level = shard_levels(key, shape, split, -0.22, 0.18) if split else 1.0
    result = jax.random.normal(key, shape, jnp.float32) * deviation * level
    return jnp.minimum(jnp.maximum(result, -reach), reach).astype(held_as)


def setup_inputs(seed: int = 0) -> dict:
    key_of = jax.random.split(jax.random.key(seed), 7)
    hidden = scatter_about(key_of[0], (TOKENS, FF), 1.0, 6.0, ((0, 8), (1, 4)))
    w_out = scatter_about(key_of[1], (D, FF), FF ** -0.5, 0.0546875, ((0, 8), (1, 4)))
    direction = scatter_about(key_of[2], (D, FF), 1.0, 6.0, ((0, 8), (1, 4)))
    targets = scatter_about(key_of[3], (TOKENS, D), 1.0, 6.0, ((0, 4), (1, 8)))
    codes = with_ends(jax.random.randint(key_of[4], (IMAGES,), 0, CODES), jax.random.fold_in(key_of[4], 1), 0, CODES - 1).astype(jnp.int32)
    code_weights = jnp.clip(jnp.exp(jax.random.uniform(key_of[5], (CODES,), jnp.float32, math.log(0.5), math.log(2.0))), 0.5, 2.0)
    return {"hidden": hidden, "w_out": w_out, "direction": direction, "targets": targets, "codes": codes, "code_weights": code_weights}


STEP = 0.5


def flip_targets(targets, codes):
    image_count = codes.shape[0]
    patch_grid = targets.reshape(image_count, GRID, GRID, targets.shape[1])
    horizontal = (codes % 2 == 1)[:, None, None, None]
    vertical = (codes // 2 == 1)[:, None, None, None]
    patch_grid = jnp.where(horizontal, patch_grid[:, :, ::-1], patch_grid)
    patch_grid = jnp.where(vertical, patch_grid[:, ::-1], patch_grid)
    return patch_grid.reshape(targets.shape)


def reference(hidden, w_out, direction, targets, codes, code_weights):
    tokens_all = hidden.shape[0]
    width = w_out.shape[0]
    block = FF // N_MP
    stacked = jnp.concatenate([w_out, direction], axis=0)

    def add_block(total, position):
        first = (position * block).astype(jnp.int32)
        left = lax.dynamic_slice_in_dim(hidden, first, block, 1)
        right = lax.dynamic_slice_in_dim(stacked, first, block, 1)
        partial_sum = lax.dot_general(left, right, (((1,), (1,)), ((), ())), preferred_element_type=jnp.float32).astype(jnp.bfloat16)
        partial_sum = lax.optimization_barrier(partial_sum)
        return total + partial_sum.astype(jnp.float32), None

    start_total = jnp.zeros((tokens_all, 2 * width), jnp.float32)
    sums, _ = lax.scan(add_block, start_total, jnp.arange(N_MP, dtype=jnp.int32))
    outputs = sums[:, :width]
    moved = sums[:, width:]
    aligned = flip_targets(targets, codes).astype(jnp.float32)
    slope = 1.0 - jnp.tanh(outputs - aligned) ** 2
    image_weight = jnp.sum(jnp.where(codes[:, None] == jnp.arange(CODES, dtype=jnp.int32)[None, :], code_weights[None, :], 0.0), axis=1)
    product = (slope * moved).reshape(codes.shape[0], PATCHES, width) * image_weight[:, None, None]
    scaled = product.reshape(tokens_all, width).astype(jnp.bfloat16)
    curvature = lax.dot_general(scaled, hidden, (((0,), (0,)), ((), ())), preferred_element_type=jnp.float32) / tokens_all
    return 2.0 * direction.astype(jnp.float32) - STEP * curvature
```

```python
import jax
import jax.numpy as jnp
from jax import lax
from jax.sharding import PartitionSpec as P

GRID = 16
PATCHES = 256


STEP = 0.5


def contract_rows(left, right):
    return lax.dot_general(
        left, right, (((0,), (0,)), ((), ())), preferred_element_type=jnp.float32
    )


def weigh_rows(sums, targets, codes, code_weights, first_row):
    row_count = targets.shape[0]
    width = targets.shape[1]
    image_count = row_count // PATCHES
    image_codes = lax.dynamic_slice_in_dim(codes, first_row // PATCHES, image_count, 0)
    patch_grid = targets.reshape(image_count, GRID, GRID, width)
    horizontal = (image_codes % 2 == 1)[:, None, None, None]
    vertical = (image_codes // 2 == 1)[:, None, None, None]
    patch_grid = jnp.where(horizontal, patch_grid[:, :, ::-1], patch_grid)
    patch_grid = jnp.where(vertical, patch_grid[:, ::-1], patch_grid)
    aligned = patch_grid.reshape(row_count, width).astype(jnp.float32)
    outputs = sums[:, :width]
    moved = sums[:, width:]
    slope = 1.0 - jnp.tanh(outputs - aligned) ** 2
    image_weight = jnp.sum(
        jnp.where(
            image_codes[:, None] == jnp.arange(code_weights.shape[0], dtype=jnp.int32)[None, :],
            code_weights[None, :],
            0.0,
        ),
        axis=1,
    )
    product = (slope * moved).reshape(image_count, PATCHES, width) * image_weight[:, None, None]
    return product.reshape(row_count, width).astype(jnp.bfloat16)


def project_rows(rows_here, stacked):
    return lax.dot_general(
        rows_here, stacked, (((1,), (1,)), ((), ())), preferred_element_type=jnp.float32
    )


def on_device_any(hidden, w_out, direction, targets, codes, code_weights):
    stacked = jnp.concatenate([w_out, direction], axis=0)
    whole = lax.all_gather(hidden, "dp", axis=0, tiled=True)
    sums = lax.psum_scatter(
        project_rows(whole, stacked).astype(jnp.bfloat16), "mp", scatter_dimension=0, tiled=True
    ).astype(jnp.float32)
    first_row = lax.axis_index("mp") * targets.shape[0]
    scaled = weigh_rows(sums, targets, codes, code_weights, first_row)
    curvature = contract_rows(lax.all_gather(scaled, "mp", axis=0, tiled=True), whole)
    return 2.0 * direction.astype(jnp.float32) - STEP * (curvature / whole.shape[0])


RING = (0, 2, 4, 6, 7, 5, 3, 1)
COUNT = len(RING)
UP = [(RING[i], RING[(i + 1) % COUNT]) for i in range(COUNT)]
DOWN = [(RING[i], RING[(i - 1) % COUNT]) for i in range(COUNT)]
CORE = [(i, i ^ 1) for i in range(4)]
ROW = [(i, i ^ 2) for i in range(4)]


def order_of(dp):
    at = RING.index(dp)
    seq = [(0, 0), (0, 1)]
    for k in range(1, COUNT // 2):
        seq += [(-k, 0), (k, 0), (-k, 1), (k, 1)]
    seq += [(COUNT // 2, 0), (COUNT // 2, 1)]
    return [2 * RING[(at + k) % COUNT] + h for k, h in seq]


ORDER = [order_of(d) for d in range(COUNT)]


def on_device(hidden, w_out, direction, targets, codes, code_weights):
    dp = lax.axis_index("dp")
    mp = lax.axis_index("mp")
    core = mp % 2
    rows, width = hidden.shape[0], w_out.shape[0]
    half, part = rows // 2, width // 2
    tokens_all = rows * COUNT

    def swap(value, pairs):
        return lax.ppermute(value, "mp", pairs)

    up, down = [(hidden[:half], hidden[half:])], [(hidden[:half], hidden[half:])]
    for k in range(1, COUNT // 2):
        up.append(tuple(lax.ppermute(v, "dp", UP) for v in up[-1]))
        down.append(tuple(lax.ppermute(v, "dp", DOWN) for v in down[-1]))
    last = (lax.ppermute(up[-1][0], "dp", UP), lax.ppermute(down[-1][1], "dp", DOWN))

    def cols(value, which):
        return lax.dynamic_slice_in_dim(value, which * part, part, 1)

    two = jnp.concatenate([cols(targets, core), swap(cols(targets, 1 - core), CORE)], axis=0)
    four = jnp.concatenate([two, swap(two, ROW)], axis=0)
    base = jnp.asarray(ORDER, jnp.int32)[dp] * half
    token = (base[:, None] + jnp.arange(half, dtype=jnp.int32)[None, :]).reshape(1, tokens_all)
    image, patch = token // PATCHES, token % PATCHES

    def look_up(table, index):
        at = jnp.arange(table.shape[0], dtype=jnp.int32)[:, None]
        return jnp.sum(jnp.where(index == at, table[:, None], 0), axis=0, keepdims=True)

    code = look_up(codes, image)
    weight = look_up(code_weights, code)
    row, col = patch // GRID, patch % GRID
    col = jnp.where(code % 2 == 1, GRID - 1 - col, col)
    row = jnp.where(code // 2 == 1, GRID - 1 - row, row)
    source = (image ^ mp) * PATCHES + row * GRID + col
    one_hot = (jnp.arange(tokens_all, dtype=jnp.int32)[:, None] == source).astype(jnp.bfloat16)
    aligned = contract_rows(four, one_hot)

    def pair_rows(which):
        return jnp.concatenate(
            [lax.dynamic_slice_in_dim(w_out, which * part, part, 0),
             lax.dynamic_slice_in_dim(direction, which * part, part, 0)], axis=0)

    stack_mine, stack_theirs = pair_rows(core), pair_rows(1 - core)

    def round_of(block, start):
        theirs = swap(project_rows(stack_theirs, block).astype(jnp.bfloat16), CORE)
        kept = project_rows(stack_mine, block).astype(jnp.bfloat16).astype(jnp.float32)
        chip = kept + theirs.astype(jnp.float32)
        sums = chip + swap(chip.astype(jnp.bfloat16), ROW).astype(jnp.float32)
        at = slice(start, start + block.shape[0])
        slope = 1.0 - jnp.tanh(sums[:part] - aligned[:, at]) ** 2
        mine = (weight[:, at] * slope * sums[part:]).astype(jnp.bfloat16)
        theirs = swap(mine, CORE)
        low, high = lax.select(core == 0, mine, theirs), lax.select(core == 0, theirs, mine)
        return jnp.concatenate([low, high], axis=0)

    blocks = [hidden]
    for k in range(1, COUNT // 2):
        blocks.append(jnp.concatenate([up[k][0], down[k][0], up[k][1], down[k][1]], axis=0))
    blocks.append(jnp.concatenate(last, axis=0))
    start, scaled = 0, []
    for block in blocks:
        scaled.append(round_of(block, start))
        start += block.shape[0]
    curvature = jnp.dot(
        jnp.concatenate(scaled, axis=1), jnp.concatenate(blocks, axis=0), preferred_element_type=jnp.float32
    )
    return 2.0 * direction.astype(jnp.float32) - STEP * (curvature / tokens_all)


def solution(mesh):
    planned = mesh.shape["dp"] == COUNT and mesh.shape["mp"] == 4
    return jax.shard_map(
        on_device if planned else on_device_any,
        mesh=mesh,
        in_specs=(P("dp", "mp"), P("dp", "mp"), P("dp", "mp"), P("mp", "dp"), P(), P()),
        out_specs=P("dp", "mp"),
        check_vma=False,
    )
```

```python
import functools

import jax
import jax.numpy as jnp
from jax import lax
from jax.experimental import pallas as pl
from jax.experimental.pallas import tpu as pltpu
from jax.sharding import PartitionSpec as P

GRID = 16
PATCHES = 256


STEP = 0.5


def contract_rows(left, right):
    return lax.dot_general(
        left, right, (((0,), (0,)), ((), ())), preferred_element_type=jnp.float32
    )


def weigh_rows(sums, targets, codes, code_weights, first_row):
    row_count = targets.shape[0]
    width = targets.shape[1]
    image_count = row_count // PATCHES
    image_codes = lax.dynamic_slice_in_dim(codes, first_row // PATCHES, image_count, 0)
    patch_grid = targets.reshape(image_count, GRID, GRID, width)
    horizontal = (image_codes % 2 == 1)[:, None, None, None]
    vertical = (image_codes // 2 == 1)[:, None, None, None]
    patch_grid = jnp.where(horizontal, patch_grid[:, :, ::-1], patch_grid)
    patch_grid = jnp.where(vertical, patch_grid[:, ::-1], patch_grid)
    aligned = patch_grid.reshape(row_count, width).astype(jnp.float32)
    outputs = sums[:, :width]
    moved = sums[:, width:]
    slope = 1.0 - jnp.tanh(outputs - aligned) ** 2
    image_weight = jnp.sum(
        jnp.where(
            image_codes[:, None] == jnp.arange(code_weights.shape[0], dtype=jnp.int32)[None, :],
            code_weights[None, :],
            0.0,
        ),
        axis=1,
    )
    product = (slope * moved).reshape(image_count, PATCHES, width) * image_weight[:, None, None]
    return product.reshape(row_count, width).astype(jnp.bfloat16)


def project_rows(rows_here, stacked):
    return lax.dot_general(
        rows_here, stacked, (((1,), (1,)), ((), ())), preferred_element_type=jnp.float32
    )


def on_device_any(hidden, w_out, direction, targets, codes, code_weights):
    stacked = jnp.concatenate([w_out, direction], axis=0)
    whole = lax.all_gather(hidden, "dp", axis=0, tiled=True)
    sums = lax.psum_scatter(
        project_rows(whole, stacked).astype(jnp.bfloat16), "mp", scatter_dimension=0, tiled=True
    ).astype(jnp.float32)
    first_row = lax.axis_index("mp") * targets.shape[0]
    scaled = weigh_rows(sums, targets, codes, code_weights, first_row)
    curvature = contract_rows(lax.all_gather(scaled, "mp", axis=0, tiled=True), whole)
    return 2.0 * direction.astype(jnp.float32) - STEP * (curvature / whole.shape[0])


RING = (0, 2, 4, 6, 7, 5, 3, 1)
COUNT = len(RING)
UP = [(RING[i], RING[(i + 1) % COUNT]) for i in range(COUNT)]
DOWN = [(RING[i], RING[(i - 1) % COUNT]) for i in range(COUNT)]
CORE = [(i, i ^ 1) for i in range(4)]
ROW = [(i, i ^ 2) for i in range(4)]


def order_of(dp):
    at = RING.index(dp)
    seq = [(0, 0), (0, 1)]
    for k in range(1, COUNT // 2):
        seq += [(-k, 0), (-k, 1), (k, 0), (k, 1)]
    seq += [(COUNT // 2, 0), (COUNT // 2, 1)]
    return [2 * RING[(at + k) % COUNT] + h for k, h in seq]


ORDER = [order_of(d) for d in range(COUNT)]


WEIGHT = 0.15


def cost(flops):
    return pl.CostEstimate(flops=int(WEIGHT * flops), bytes_accessed=0, transcendentals=0)


IN_VMEM = pl.BlockSpec(memory_space=pltpu.VMEM)


def project_kernel(wanted, count, which_ref, w_ref, d_ref, *refs):
    parts, outs, block = refs[:count], refs[count:-1], refs[-1]
    part = w_ref.shape[0] // 2
    row = 0
    for ref in parts:
        block[row : row + ref.shape[0], :] = ref[...]
        row += ref.shape[0]
    for flip, out in zip(wanted, outs):
        which = which_ref[0] if flip == 0 else 1 - which_ref[0]
        rows = pl.ds(pl.multiple_of(which * part, part), part)
        for at, source in enumerate((w_ref, d_ref)):
            out[at * part : (at + 1) * part, :] = project_rows(source[rows, :], block[...]).astype(out.dtype)


def project(core, w_out, direction, parts, wanted):
    count = sum(v.shape[0] for v in parts)
    width, depth = w_out.shape
    return pl.pallas_call(
        functools.partial(project_kernel, wanted, len(parts)),
        out_shape=[jax.ShapeDtypeStruct((width, count), jnp.bfloat16) for _ in wanted]
        + [jax.ShapeDtypeStruct((count, depth), jnp.bfloat16)],
        in_specs=[pl.BlockSpec(memory_space=pltpu.SMEM)] + [IN_VMEM] * (2 + len(parts)),
        out_specs=[IN_VMEM] * (len(wanted) + 1),
        compiler_params=pltpu.CompilerParams(vmem_limit_bytes=20 * 2**20),
        cost_estimate=cost(2 * len(wanted) * width * max(count, 256) * depth),
        name="project",
    )(core, w_out, direction, *parts)


def contract_kernel(count, step, tile, which_ref, base_ref, *refs):
    terms, out = [refs[3 * i : 3 * i + 3] for i in range(count)], refs[3 * count]
    width, depth = base_ref.shape
    part = width // 2
    first = base_ref.dtype == jnp.bfloat16
    if not first:
        buffer, sem = refs[3 * count + 1 :]

    def copy_of(i):
        columns = pl.ds(pl.multiple_of(i * tile, tile), tile)
        return pltpu.make_async_copy(buffer.at[i % 2], out.at[:, columns], sem.at[i % 2])

    for i in range(depth // tile):
        columns = slice(i * tile, (i + 1) * tile)
        if not first and i >= 2:
            copy_of(i - 2).wait()
        for flip in (0, 1):
            which = which_ref[0] if flip == 0 else 1 - which_ref[0]
            rows = pl.ds(pl.multiple_of(which * part, part), part)
            total = sum(
                jnp.dot(term[flip][...], term[2][:, columns], preferred_element_type=jnp.float32) for term in terms
            )
            if first:
                out[rows, columns] = 2.0 * base_ref[rows, columns].astype(jnp.float32) - step * total
            else:
                buffer[i % 2, rows, :] = base_ref[rows, columns] - step * total
        if not first:
            copy_of(i).start()
    if not first:
        for i in range(max(0, depth // tile - 2), depth // tile):
            copy_of(i).wait()


def contract(core, base, terms, step):
    width, depth = base.shape
    first = base.dtype == jnp.bfloat16
    tile = 512
    while depth % tile:
        tile //= 2
    return pl.pallas_call(
        functools.partial(contract_kernel, len(terms), step, tile),
        out_shape=jax.ShapeDtypeStruct((width, depth), jnp.float32),
        in_specs=[pl.BlockSpec(memory_space=pltpu.SMEM)] + [IN_VMEM] * (1 + 3 * len(terms)),
        out_specs=IN_VMEM if first else pl.BlockSpec(memory_space=pl.ANY),
        scratch_shapes=[]
        if first
        else [pltpu.VMEM((2, width, tile), jnp.float32), pltpu.SemaphoreType.DMA((2,))],
        compiler_params=pltpu.CompilerParams(vmem_limit_bytes=20 * 2**20),
        cost_estimate=cost(2 * width * depth * sum(term[2].shape[0] for term in terms)),
        name="contract",
    )(core, base, *[v for term in terms for v in term])


def on_device(hidden, w_out, direction, targets, codes, code_weights):
    dp = lax.axis_index("dp")
    mp = lax.axis_index("mp")
    core = mp % 2
    rows, width = hidden.shape[0], w_out.shape[0]
    half, part = rows // 2, width // 2
    tokens_all = rows * COUNT

    def swap(value, pairs):
        return lax.ppermute(value, "mp", pairs)

    def gate(*values):
        return lax.optimization_barrier(values)

    def step(pair):
        return lax.ppermute(pair[0], "dp", UP), lax.ppermute(pair[1], "dp", DOWN)

    def cols(value, which):
        return lax.dynamic_slice_in_dim(value, which * part, part, 1)

    two = jnp.concatenate([cols(targets, core), swap(cols(targets, 1 - core), CORE)], axis=0)
    other = swap(two, ROW)
    base = jnp.asarray(ORDER, jnp.int32)[dp] * half
    token = (base[:, None] + jnp.arange(half, dtype=jnp.int32)[None, :]).reshape(1, tokens_all)
    image, patch = token // PATCHES, token % PATCHES

    def look_up(table, index):
        at = jnp.arange(table.shape[0], dtype=jnp.int32)[:, None]
        return jnp.sum(jnp.where(index == at, table[:, None], 0), axis=0, keepdims=True)

    code = look_up(codes, image)
    weight = look_up(code_weights, code)
    row, col = patch // GRID, patch % GRID
    col = jnp.where(code % 2 == 1, GRID - 1 - col, col)
    row = jnp.where(code // 2 == 1, GRID - 1 - row, row)
    source = (image ^ mp) * PATCHES + row * GRID + col
    one_hot = (jnp.arange(tokens_all, dtype=jnp.int32)[:, None] == source).astype(jnp.bfloat16)

    aligned = contract_rows(jnp.concatenate([two, other], axis=0), one_hot)
    one = core[None]

    def add(kept, theirs):
        return kept.astype(jnp.float32) + theirs.astype(jnp.float32)

    def over_rows(chip):
        return swap(chip.astype(jnp.bfloat16), ROW)

    def weigh(chip, across, start):
        sums = add(chip, across)
        at = slice(start, start + sums.shape[1])
        slope = 1.0 - jnp.tanh(sums[:part] - aligned[:, at]) ** 2
        mine = (weight[:, at] * slope * sums[part:]).astype(jnp.bfloat16)
        return mine, swap(mine, CORE)

    hop1 = step((hidden, hidden))
    theirs0, kept0, _ = project(one, w_out, direction, [hidden], (1, 0))
    chip0 = add(kept0, swap(theirs0, CORE))
    across0 = over_rows(chip0)

    hop2 = step(hop1)
    theirs1, kept1, block1 = project(one, w_out, direction, hop1, (1, 0))
    chip1 = add(kept1, swap(theirs1, CORE))
    across1 = over_rows(chip1)
    *hop2, kept1 = gate(*hop2, kept1)
    hop3 = step(hop2)
    theirs2, kept2, block2 = project(one, w_out, direction, hop2, (1, 0))
    chip2 = add(kept2, swap(theirs2, CORE))
    across2 = over_rows(chip2)
    scaled0 = weigh(chip0, across0, 0)
    *hop3, kept2 = gate(*hop3, kept2)
    hop4 = step((hop3[0][:half], hop3[1][half:]))
    theirs3, kept3, block3 = project(one, w_out, direction, hop3, (1, 0))
    chip3 = add(kept3, swap(theirs3, CORE))
    across3 = over_rows(chip3)
    scaled1 = weigh(chip1, across1, rows)
    *hop4, kept3 = gate(*hop4, kept3)
    theirs4, block4 = project(one, w_out, direction, hop4, (1,))
    theirs4 = swap(theirs4, CORE)
    kept4, _ = project(one, w_out, direction, hop4, (0,))
    chip4 = add(kept4, theirs4)
    across4 = over_rows(chip4)
    scaled2 = weigh(chip2, across2, 3 * rows)
    total = contract(one, direction, [(*scaled0, hidden), (*scaled1, block1), (*scaled2, block2)], STEP / tokens_all)
    scaled3 = weigh(chip3, across3, 5 * rows)
    scaled4 = weigh(chip4, across4, 7 * rows)
    return contract(one, total, [(*scaled3, block3), (*scaled4, block4)], STEP / tokens_all)


def solution(mesh):
    planned = mesh.shape["dp"] == COUNT and mesh.shape["mp"] == 4
    return jax.shard_map(
        on_device if planned else on_device_any,
        mesh=mesh,
        in_specs=(P("dp", "mp"), P("dp", "mp"), P("dp", "mp"), P("mp", "dp"), P(), P()),
        out_specs=P("dp", "mp"),
        check_vma=False,
    )
```

```python
import functools

import jax
import jax.numpy as jnp
from jax import lax
from jax.experimental import pallas as pl
from jax.experimental.pallas import tpu as pltpu
from jax.sharding import PartitionSpec as P

GRID = 16
PATCHES = 256


STEP = 0.5


def contract_rows(left, right):
    return lax.dot_general(
        left, right, (((0,), (0,)), ((), ())), preferred_element_type=jnp.float32
    )


def weigh_rows(sums, targets, codes, code_weights, first_row):
    row_count = targets.shape[0]
    width = targets.shape[1]
    image_count = row_count // PATCHES
    image_codes = lax.dynamic_slice_in_dim(codes, first_row // PATCHES, image_count, 0)
    patch_grid = targets.reshape(image_count, GRID, GRID, width)
    horizontal = (image_codes % 2 == 1)[:, None, None, None]
    vertical = (image_codes // 2 == 1)[:, None, None, None]
    patch_grid = jnp.where(horizontal, patch_grid[:, :, ::-1], patch_grid)
    patch_grid = jnp.where(vertical, patch_grid[:, ::-1], patch_grid)
    aligned = patch_grid.reshape(row_count, width).astype(jnp.float32)
    outputs = sums[:, :width]
    moved = sums[:, width:]
    slope = 1.0 - jnp.tanh(outputs - aligned) ** 2
    image_weight = jnp.sum(
        jnp.where(
            image_codes[:, None] == jnp.arange(code_weights.shape[0], dtype=jnp.int32)[None, :],
            code_weights[None, :],
            0.0,
        ),
        axis=1,
    )
    product = (slope * moved).reshape(image_count, PATCHES, width) * image_weight[:, None, None]
    return product.reshape(row_count, width).astype(jnp.bfloat16)


def project_rows(rows_here, stacked):
    return lax.dot_general(
        rows_here, stacked, (((1,), (1,)), ((), ())), preferred_element_type=jnp.float32
    )


def on_device_any(hidden, w_out, direction, targets, codes, code_weights):
    stacked = jnp.concatenate([w_out, direction], axis=0)
    whole = lax.all_gather(hidden, "dp", axis=0, tiled=True)
    sums = lax.psum_scatter(
        project_rows(whole, stacked).astype(jnp.bfloat16), "mp", scatter_dimension=0, tiled=True
    ).astype(jnp.float32)
    first_row = lax.axis_index("mp") * targets.shape[0]
    scaled = weigh_rows(sums, targets, codes, code_weights, first_row)
    curvature = contract_rows(lax.all_gather(scaled, "mp", axis=0, tiled=True), whole)
    return 2.0 * direction.astype(jnp.float32) - STEP * (curvature / whole.shape[0])


RING = (0, 2, 4, 6, 7, 5, 3, 1)
COUNT = len(RING)
UP = [(RING[i], RING[(i + 1) % COUNT]) for i in range(COUNT)]
DOWN = [(RING[i], RING[(i - 1) % COUNT]) for i in range(COUNT)]
CORE = [(i, i ^ 1) for i in range(4)]
ROW = [(i, i ^ 2) for i in range(4)]


def order_of(dp):
    at = RING.index(dp)
    seq = [(0, 0), (0, 1)]
    for k in range(1, COUNT // 2):
        seq += [(-k, 0), (-k, 1), (k, 0), (k, 1)]
    seq += [(COUNT // 2, 0), (COUNT // 2, 1)]
    return [2 * RING[(at + k) % COUNT] + h for k, h in seq]


ORDER = [order_of(d) for d in range(COUNT)]


WEIGHT = 0.15


def cost(flops):
    return pl.CostEstimate(flops=int(WEIGHT * flops), bytes_accessed=0, transcendentals=0)


IN_VMEM = pl.BlockSpec(memory_space=pltpu.VMEM)


def project_kernel(wanted, count, which_ref, w_ref, d_ref, *refs):
    parts, outs, block = refs[:count], refs[count:-1], refs[-1]
    part = w_ref.shape[0] // 2
    row = 0
    for ref in parts:
        block[row : row + ref.shape[0], :] = ref[...]
        row += ref.shape[0]
    for flip, out in zip(wanted, outs):
        which = which_ref[0] if flip == 0 else 1 - which_ref[0]
        rows = pl.ds(pl.multiple_of(which * part, part), part)
        for at, source in enumerate((w_ref, d_ref)):
            out[at * part : (at + 1) * part, :] = project_rows(source[rows, :], block[...]).astype(out.dtype)


def project(core, w_out, direction, parts, wanted):
    count = sum(v.shape[0] for v in parts)
    width, depth = w_out.shape
    return pl.pallas_call(
        functools.partial(project_kernel, wanted, len(parts)),
        out_shape=[jax.ShapeDtypeStruct((width, count), jnp.bfloat16) for _ in wanted]
        + [jax.ShapeDtypeStruct((count, depth), jnp.bfloat16)],
        in_specs=[pl.BlockSpec(memory_space=pltpu.SMEM)] + [IN_VMEM] * (2 + len(parts)),
        out_specs=[IN_VMEM] * (len(wanted) + 1),
        compiler_params=pltpu.CompilerParams(vmem_limit_bytes=20 * 2**20),
        cost_estimate=cost(2 * len(wanted) * width * max(count, 256) * depth),
        name="project",
    )(core, w_out, direction, *parts)


def contract_kernel(count, step, tile, last, which_ref, base_ref, *refs):
    terms, out = [refs[3 * i : 3 * i + 3] for i in range(count)], refs[3 * count]
    width, depth = base_ref.shape
    part = width // 2
    tiles = depth // tile
    if last:
        buffer, sem = refs[3 * count + 1 :]

    def copy_of(i):
        return pltpu.make_async_copy(buffer.at[i], out.at[:, i * tile : (i + 1) * tile], sem.at[i])

    for i in range(tiles):
        columns = slice(i * tile, (i + 1) * tile)
        for flip in (0, 1):
            which = which_ref[0] if flip == 0 else 1 - which_ref[0]
            rows = pl.ds(pl.multiple_of(which * part, part), part)
            total = sum(
                jnp.dot(term[flip][...], term[2][:, columns], preferred_element_type=jnp.float32) for term in terms
            )
            base = base_ref[rows, columns]
            if base.dtype == jnp.bfloat16:
                base = 2.0 * base.astype(jnp.float32)
            if last:
                buffer[i, rows, :] = base - step * total
            else:
                out[rows, columns] = base - step * total
        if last:
            copy_of(i).start()
    if last:
        for i in range(tiles):
            copy_of(i).wait()


def contract(core, base, terms, step, last):
    width, depth = base.shape
    tile = 512
    while depth % tile:
        tile //= 2
    tiles = depth // tile
    return pl.pallas_call(
        functools.partial(contract_kernel, len(terms), step, tile, last),
        out_shape=jax.ShapeDtypeStruct((width, depth), jnp.float32),
        in_specs=[pl.BlockSpec(memory_space=pltpu.SMEM)] + [IN_VMEM] * (1 + 3 * len(terms)),
        out_specs=pl.BlockSpec(memory_space=pl.ANY) if last else IN_VMEM,
        scratch_shapes=[pltpu.VMEM((tiles, width, tile), jnp.float32), pltpu.SemaphoreType.DMA((tiles,))] if last else [],
        input_output_aliases={1: 0} if base.dtype == jnp.float32 and not last else {},
        compiler_params=pltpu.CompilerParams(vmem_limit_bytes=20 * 2**20),
        cost_estimate=cost(2 * width * depth * sum(term[2].shape[0] for term in terms)),
        name="contract",
    )(core, base, *[v for term in terms for v in term])


def on_device(hidden, w_out, direction, targets, codes, code_weights):
    dp = lax.axis_index("dp")
    mp = lax.axis_index("mp")
    core = mp % 2
    rows, width = hidden.shape[0], w_out.shape[0]
    half, part = rows // 2, width // 2
    tokens_all = rows * COUNT

    def swap(value, pairs):
        return lax.ppermute(value, "mp", pairs)

    def gate(*values):
        return lax.optimization_barrier(values)

    def step(pair):
        return lax.ppermute(pair[0], "dp", UP), lax.ppermute(pair[1], "dp", DOWN)

    def cols(value, which):
        return lax.dynamic_slice_in_dim(value, which * part, part, 1)

    two = jnp.concatenate([cols(targets, core), swap(cols(targets, 1 - core), CORE)], axis=0)
    other = swap(two, ROW)
    base = jnp.asarray(ORDER, jnp.int32)[dp] * half
    token = (base[:, None] + jnp.arange(half, dtype=jnp.int32)[None, :]).reshape(1, tokens_all)
    image, patch = token // PATCHES, token % PATCHES

    def look_up(table, index):
        at = jnp.arange(table.shape[0], dtype=jnp.int32)[:, None]
        return jnp.sum(jnp.where(index == at, table[:, None], 0), axis=0, keepdims=True)

    code = look_up(codes, image)
    weight = look_up(code_weights, code)
    row, col = patch // GRID, patch % GRID
    col = jnp.where(code % 2 == 1, GRID - 1 - col, col)
    row = jnp.where(code // 2 == 1, GRID - 1 - row, row)
    source = (image ^ mp) * PATCHES + row * GRID + col
    one_hot = (jnp.arange(tokens_all, dtype=jnp.int32)[:, None] == source).astype(jnp.bfloat16)

    one = core[None]

    def align(other):
        return contract_rows(jnp.concatenate([two, other], axis=0), one_hot)

    def add(kept, theirs):
        return kept.astype(jnp.float32) + theirs.astype(jnp.float32)

    def over_rows(chip):
        return swap(chip.astype(jnp.bfloat16), ROW)

    def weigh(aligned, chip, across, start):
        sums = add(chip, across)
        at = slice(start, start + sums.shape[1])
        slope = 1.0 - jnp.tanh(sums[:part] - aligned[:, at]) ** 2
        mine = (weight[:, at] * slope * sums[part:]).astype(jnp.bfloat16)
        return mine, swap(mine, CORE)

    hop1 = step((hidden, hidden))
    theirs0, kept0, _ = project(one, w_out, direction, [hidden], (1, 0))
    chip0 = add(kept0, swap(theirs0, CORE))
    across0 = over_rows(chip0)

    hop2 = step(hop1)
    theirs1, kept1, block1 = project(one, w_out, direction, hop1, (1, 0))
    chip1 = add(kept1, swap(theirs1, CORE))
    across1 = over_rows(chip1)
    *hop2, kept1, chip0, across0, other = gate(*hop2, kept1, chip0, across0, other)
    aligned = align(other)
    hop3 = step(hop2)
    theirs2, kept2, block2 = project(one, w_out, direction, hop2, (1, 0))
    chip2 = add(kept2, swap(theirs2, CORE))
    across2 = over_rows(chip2)
    scaled0 = weigh(aligned, chip0, across0, 0)
    *hop3, kept2, chip1, across1 = gate(*hop3, kept2, chip1, across1)
    hop4 = step((hop3[0][:half], hop3[1][half:]))
    theirs3, kept3, block3 = project(one, w_out, direction, hop3, (1, 0))
    theirs3 = swap(theirs3, CORE)
    scaled1 = weigh(aligned, chip1, across1, rows)
    *hop4, kept3, chip2, across2 = gate(*hop4, kept3, chip2, across2)
    scaled2 = weigh(aligned, chip2, across2, 3 * rows)
    theirs3, mine2 = gate(theirs3, scaled2[0])
    scaled2 = (mine2, scaled2[1])
    chip3 = add(kept3, theirs3)
    across3 = over_rows(chip3)
    theirs4, block4 = project(one, w_out, direction, hop4, (1,))
    theirs4 = swap(theirs4, CORE)
    kept4, _ = project(one, w_out, direction, hop4, (0,))
    chip4 = add(kept4, theirs4)
    across4 = over_rows(chip4)
    share = STEP / tokens_all
    block2, chip4 = gate(block2, chip4)
    total = contract(one, direction, [(*scaled0, hidden), (*scaled1, block1), (*scaled2, block2)], share, False)
    total, chip3 = gate(total, chip3)
    scaled3 = weigh(aligned, chip3, across3, 5 * rows)
    mine3, chip4 = gate(scaled3[0], chip4)
    scaled4 = weigh(aligned, chip4, across4, 7 * rows)
    return contract(one, total, [(mine3, scaled3[1], block3), (*scaled4, block4)], share, True)


def solution(mesh):
    planned = mesh.shape["dp"] == COUNT and mesh.shape["mp"] == 4
    return jax.shard_map(
        on_device if planned else on_device_any,
        mesh=mesh,
        in_specs=(P("dp", "mp"), P("dp", "mp"), P("dp", "mp"), P("mp", "dp"), P(), P()),
        out_specs=P("dp", "mp"),
        check_vma=False,
    )
```

```python
import functools

import jax
import jax.numpy as jnp
from jax import lax
from jax.experimental import pallas as pl
from jax.experimental.pallas import tpu as pltpu
from jax.sharding import PartitionSpec as P

GRID = 16
PATCHES = 256


STEP = 0.5


def contract_rows(left, right):
    return lax.dot_general(
        left, right, (((0,), (0,)), ((), ())), preferred_element_type=jnp.float32
    )


def weigh_rows(sums, targets, codes, code_weights, first_row):
    row_count = targets.shape[0]
    width = targets.shape[1]
    image_count = row_count // PATCHES
    image_codes = lax.dynamic_slice_in_dim(codes, first_row // PATCHES, image_count, 0)
    patch_grid = targets.reshape(image_count, GRID, GRID, width)
    horizontal = (image_codes % 2 == 1)[:, None, None, None]
    vertical = (image_codes // 2 == 1)[:, None, None, None]
    patch_grid = jnp.where(horizontal, patch_grid[:, :, ::-1], patch_grid)
    patch_grid = jnp.where(vertical, patch_grid[:, ::-1], patch_grid)
    aligned = patch_grid.reshape(row_count, width).astype(jnp.float32)
    outputs = sums[:, :width]
    moved = sums[:, width:]
    slope = 1.0 - jnp.tanh(outputs - aligned) ** 2
    image_weight = jnp.sum(
        jnp.where(
            image_codes[:, None] == jnp.arange(code_weights.shape[0], dtype=jnp.int32)[None, :],
            code_weights[None, :],
            0.0,
        ),
        axis=1,
    )
    product = (slope * moved).reshape(image_count, PATCHES, width) * image_weight[:, None, None]
    return product.reshape(row_count, width).astype(jnp.bfloat16)


def project_rows(rows_here, stacked):
    return lax.dot_general(
        rows_here, stacked, (((1,), (1,)), ((), ())), preferred_element_type=jnp.float32
    )


def on_device_any(hidden, w_out, direction, targets, codes, code_weights):
    stacked = jnp.concatenate([w_out, direction], axis=0)
    whole = lax.all_gather(hidden, "dp", axis=0, tiled=True)
    sums = lax.psum_scatter(
        project_rows(whole, stacked).astype(jnp.bfloat16), "mp", scatter_dimension=0, tiled=True
    ).astype(jnp.float32)
    first_row = lax.axis_index("mp") * targets.shape[0]
    scaled = weigh_rows(sums, targets, codes, code_weights, first_row)
    curvature = contract_rows(lax.all_gather(scaled, "mp", axis=0, tiled=True), whole)
    return 2.0 * direction.astype(jnp.float32) - STEP * (curvature / whole.shape[0])


RING = (0, 2, 4, 6, 7, 5, 3, 1)
COUNT = len(RING)
UP = [(RING[i], RING[(i + 1) % COUNT]) for i in range(COUNT)]
DOWN = [(RING[i], RING[(i - 1) % COUNT]) for i in range(COUNT)]
CORE = [(i, i ^ 1) for i in range(4)]
ROW = [(i, i ^ 2) for i in range(4)]


def order_of(dp):
    at = RING.index(dp)
    seq = [(0, 0), (0, 1)]
    for k in range(1, COUNT // 2):
        seq += [(-k, 0), (-k, 1), (k, 0), (k, 1)]
    seq += [(COUNT // 2, 0), (COUNT // 2, 1)]
    return [2 * RING[(at + k) % COUNT] + h for k, h in seq]


ORDER = [order_of(d) for d in range(COUNT)]


WEIGHT = 0.15


def cost(flops):
    return pl.CostEstimate(flops=int(WEIGHT * flops), bytes_accessed=0, transcendentals=0)


IN_VMEM = pl.BlockSpec(memory_space=pltpu.VMEM)


KEEP, GIVE = (0, (0, 1)), (1, (0, 1))


def project_kernel(wanted, count, which_ref, w_ref, d_ref, *refs):
    parts, outs = refs[:count], refs[count : count + len(wanted)]
    part = w_ref.shape[0] // 2
    block, row = refs[-1] if count > 1 else parts[0], 0
    for ref in parts if count > 1 else ():
        block[row : row + ref.shape[0], :] = ref[...]
        row += ref.shape[0]
    for (flip, sources), out in zip(wanted, outs):
        which = which_ref[0] if flip == 0 else 1 - which_ref[0]
        rows = pl.ds(pl.multiple_of(which * part, part), part)
        for at, source in enumerate(sources):
            values = project_rows((w_ref, d_ref)[source][rows, :], block[...])
            out[at * part : (at + 1) * part, :] = values.astype(out.dtype)


def project(core, w_out, direction, parts, wanted):
    count = sum(v.shape[0] for v in parts)
    width, depth = w_out.shape
    return pl.pallas_call(
        functools.partial(project_kernel, wanted, len(parts)),
        out_shape=[jax.ShapeDtypeStruct((width // 2 * len(sources), count), jnp.bfloat16) for _, sources in wanted]
        + [jax.ShapeDtypeStruct((count, depth), jnp.bfloat16)] * (len(parts) > 1),
        in_specs=[pl.BlockSpec(memory_space=pltpu.SMEM)] + [IN_VMEM] * (2 + len(parts)),
        out_specs=[IN_VMEM] * (len(wanted) + (len(parts) > 1)),
        compiler_params=pltpu.CompilerParams(vmem_limit_bytes=20 * 2**20),
        cost_estimate=cost(sum(len(sources) for _, sources in wanted) * width * max(count, 256) * depth),
        name="project",
    )(core, w_out, direction, *parts)


def merge_kernel(kept_ref, *refs):
    *pieces, chip, sent = refs
    row = 0
    for piece in pieces:
        rows = slice(row, row + piece.shape[0])
        total = kept_ref[rows, :].astype(jnp.float32) + piece[...].astype(jnp.float32)
        chip[rows, :] = total
        sent[rows, :] = total.astype(sent.dtype)
        row += piece.shape[0]


def merge(kept, *pieces):
    return pl.pallas_call(
        merge_kernel,
        out_shape=[jax.ShapeDtypeStruct(kept.shape, jnp.float32), jax.ShapeDtypeStruct(kept.shape, jnp.bfloat16)],
        in_specs=[IN_VMEM] * (1 + len(pieces)),
        out_specs=[IN_VMEM] * 2,
        compiler_params=pltpu.CompilerParams(vmem_limit_bytes=6 * 2**20),
        cost_estimate=cost(0),
        name="merge",
    )(kept, *pieces)


def contract_kernel(count, step, tile, flips, last, which_ref, base_ref, *refs):
    size = len(flips) + 1
    terms, refs = [refs[size * i : size * i + size] for i in range(count)], refs[size * count :]
    width, depth = base_ref.shape
    part = width // 2
    tiles = depth // tile
    if last:
        *_, out, buffer, sem = refs
    else:
        (out,) = refs

    def rows_of(flip):
        which = which_ref[0] if flip == 0 else 1 - which_ref[0]
        return pl.ds(pl.multiple_of(which * part, part), part)

    def copy_of(i, flip):
        columns = slice(i * tile, (i + 1) * tile)
        return pltpu.make_async_copy(buffer.at[i], out.at[rows_of(flip), columns], sem.at[i])

    for i in range(tiles):
        columns = slice(i * tile, (i + 1) * tile)
        for at, flip in enumerate(flips):
            rows = rows_of(flip)
            total = sum(
                jnp.dot(term[at][...], term[-1][:, columns], preferred_element_type=jnp.float32) for term in terms
            )
            base = base_ref[rows, columns]
            if base.dtype == jnp.bfloat16:
                base = 2.0 * base.astype(jnp.float32)
            if last:
                buffer[i, :, :] = base - step * total
            else:
                out[rows, columns] = base - step * total
        if last:
            copy_of(i, flips[0]).start()
    if last:
        for i in range(tiles):
            copy_of(i, flips[0]).wait()


def contract(core, base, terms, step, flips=(0, 1), last=False, into=None):
    width, depth = base.shape
    tile = 512
    while depth % tile:
        tile //= 2
    tiles = depth // tile
    operands = [v for term in terms for v in term]
    held = [] if into is None else [into]
    return pl.pallas_call(
        functools.partial(contract_kernel, len(terms), step, tile, flips, last),
        out_shape=jax.ShapeDtypeStruct((width, depth), jnp.float32),
        in_specs=[pl.BlockSpec(memory_space=pltpu.SMEM)] + [IN_VMEM] * (1 + len(operands)) + [pl.BlockSpec(memory_space=pl.ANY)] * len(held),
        out_specs=pl.BlockSpec(memory_space=pl.ANY) if last else IN_VMEM,
        scratch_shapes=[pltpu.VMEM((tiles, width // 2, tile), jnp.float32), pltpu.SemaphoreType.DMA((tiles,))] if last else [],
        input_output_aliases={2 + len(operands): 0} if held else {},
        compiler_params=pltpu.CompilerParams(vmem_limit_bytes=20 * 2**20),
        cost_estimate=cost(2 * width * depth * sum(term[-1].shape[0] for term in terms)),
        name="contract",
    )(core, base, *operands, *held)


def on_device(hidden, w_out, direction, targets, codes, code_weights):
    dp = lax.axis_index("dp")
    mp = lax.axis_index("mp")
    core = mp % 2
    rows, width = hidden.shape[0], w_out.shape[0]
    half, part = rows // 2, width // 2
    tokens_all = rows * COUNT

    def swap(value, pairs):
        return lax.ppermute(value, "mp", pairs)

    def gate(*values):
        return lax.optimization_barrier(values)

    def step(pair):
        return lax.ppermute(pair[0], "dp", UP), lax.ppermute(pair[1], "dp", DOWN)

    def cols(value, which):
        return lax.dynamic_slice_in_dim(value, which * part, part, 1)

    two = jnp.concatenate([cols(targets, core), swap(cols(targets, 1 - core), CORE)], axis=0)
    other = swap(two, ROW)
    base = jnp.asarray(ORDER, jnp.int32)[dp] * half
    token = (base[:, None] + jnp.arange(half, dtype=jnp.int32)[None, :]).reshape(1, tokens_all)
    image, patch = token // PATCHES, token % PATCHES

    def look_up(table, index):
        at = jnp.arange(table.shape[0], dtype=jnp.int32)[:, None]
        return jnp.sum(jnp.where(index == at, table[:, None], 0), axis=0, keepdims=True)

    code = look_up(codes, image)
    weight = look_up(code_weights, code)
    row, col = patch // GRID, patch % GRID
    col = jnp.where(code % 2 == 1, GRID - 1 - col, col)
    row = jnp.where(code // 2 == 1, GRID - 1 - row, row)
    source = (image ^ mp) * PATCHES + row * GRID + col
    one_hot = (jnp.arange(tokens_all, dtype=jnp.int32)[:, None] == source).astype(jnp.bfloat16)

    one = core[None]

    def align(other):
        return contract_rows(jnp.concatenate([two, other], axis=0), one_hot)

    def add(kept, theirs):
        return kept.astype(jnp.float32) + theirs.astype(jnp.float32)

    def over_rows(chip):
        return swap(chip.astype(jnp.bfloat16), ROW)

    def weigh(aligned, chip, across, start):
        sums = add(chip, across)
        at = slice(start, start + sums.shape[1])
        slope = 1.0 - jnp.tanh(sums[:part] - aligned[:, at]) ** 2
        mine = (weight[:, at] * slope * sums[part:]).astype(jnp.bfloat16)
        return mine, swap(mine, CORE)

    hop1 = step((hidden, hidden))
    theirs0, kept0 = project(one, w_out, direction, [hidden], (GIVE, KEEP))
    chip0 = add(kept0, swap(theirs0, CORE))
    across0 = over_rows(chip0)

    hop2 = step(hop1)
    theirs1, kept1, block1 = project(one, w_out, direction, hop1, (GIVE, KEEP))
    chip1 = add(kept1, swap(theirs1, CORE))
    across1 = over_rows(chip1)
    *hop2, kept1, chip0, across0, other = gate(*hop2, kept1, chip0, across0, other)
    aligned = align(other)
    hop3 = step(hop2)
    theirs2, kept2, block2 = project(one, w_out, direction, hop2, (GIVE, KEEP))
    chip2 = add(kept2, swap(theirs2, CORE))
    across2 = over_rows(chip2)
    scaled0 = weigh(aligned, chip0, across0, 0)
    *hop3, kept2, chip1, across1 = gate(*hop3, kept2, chip1, across1)
    hop4 = step((hop3[0][:half], hop3[1][half:]))
    *theirs3, kept3, block3 = project(one, w_out, direction, hop3, ((1, (0,)), (1, (1,)), KEEP))
    chip3, sent3 = merge(kept3, *[swap(v, CORE) for v in theirs3])
    across3 = swap(sent3, ROW)
    *hop4, kept3, chip2, across2, chip1 = gate(*hop4, kept3, chip2, across2, chip1)
    scaled1 = weigh(aligned, chip1, across1, rows)
    theirs4, block4 = project(one, w_out, direction, hop4, (GIVE,))
    theirs4 = swap(theirs4, CORE)
    (kept4,) = project(one, w_out, direction, [block4], (KEEP,))
    chip4 = add(kept4, theirs4)
    across4 = over_rows(chip4)
    share = STEP / tokens_all
    scaled2 = weigh(aligned, chip2, across2, 3 * rows)
    block2, chip4 = gate(block2, chip4)
    total = contract(one, direction, [(*scaled0, hidden), (*scaled1, block1), (*scaled2, block2)], share)
    total, chip3 = gate(total, chip3)
    scaled3 = weigh(aligned, chip3, across3, 5 * rows)
    mine3, chip4 = gate(scaled3[0], chip4)
    scaled4 = weigh(aligned, chip4, across4, 7 * rows)
    result = contract(one, total, [(mine3, block3), (scaled4[0], block4)], share, (0,), True)
    terms = [(scaled3[1], block3), (scaled4[1], block4)]
    return contract(one, total, terms, share, (1,), True, result)


def solution(mesh):
    planned = mesh.shape["dp"] == COUNT and mesh.shape["mp"] == 4
    return jax.shard_map(
        on_device if planned else on_device_any,
        mesh=mesh,
        in_specs=(P("dp", "mp"), P("dp", "mp"), P("dp", "mp"), P("mp", "dp"), P(), P()),
        out_specs=P("dp", "mp"),
        check_vma=False,
    )
```

```python
import functools

import jax
import jax.numpy as jnp
from jax import lax
from jax.experimental import pallas as pl
from jax.experimental.pallas import tpu as pltpu
from jax.sharding import PartitionSpec as P

GRID = 16
PATCHES = 256


STEP = 0.5


def contract_rows(left, right):
    return lax.dot_general(
        left, right, (((0,), (0,)), ((), ())), preferred_element_type=jnp.float32
    )


def weigh_rows(sums, targets, codes, code_weights, first_row):
    row_count = targets.shape[0]
    width = targets.shape[1]
    image_count = row_count // PATCHES
    image_codes = lax.dynamic_slice_in_dim(codes, first_row // PATCHES, image_count, 0)
    patch_grid = targets.reshape(image_count, GRID, GRID, width)
    horizontal = (image_codes % 2 == 1)[:, None, None, None]
    vertical = (image_codes // 2 == 1)[:, None, None, None]
    patch_grid = jnp.where(horizontal, patch_grid[:, :, ::-1], patch_grid)
    patch_grid = jnp.where(vertical, patch_grid[:, ::-1], patch_grid)
    aligned = patch_grid.reshape(row_count, width).astype(jnp.float32)
    outputs = sums[:, :width]
    moved = sums[:, width:]
    slope = 1.0 - jnp.tanh(outputs - aligned) ** 2
    image_weight = jnp.sum(
        jnp.where(
            image_codes[:, None] == jnp.arange(code_weights.shape[0], dtype=jnp.int32)[None, :],
            code_weights[None, :],
            0.0,
        ),
        axis=1,
    )
    product = (slope * moved).reshape(image_count, PATCHES, width) * image_weight[:, None, None]
    return product.reshape(row_count, width).astype(jnp.bfloat16)


def project_rows(rows_here, stacked):
    return lax.dot_general(
        rows_here, stacked, (((1,), (1,)), ((), ())), preferred_element_type=jnp.float32
    )


def on_device_any(hidden, w_out, direction, targets, codes, code_weights):
    stacked = jnp.concatenate([w_out, direction], axis=0)
    whole = lax.all_gather(hidden, "dp", axis=0, tiled=True)
    sums = lax.psum_scatter(
        project_rows(whole, stacked).astype(jnp.bfloat16), "mp", scatter_dimension=0, tiled=True
    ).astype(jnp.float32)
    first_row = lax.axis_index("mp") * targets.shape[0]
    scaled = weigh_rows(sums, targets, codes, code_weights, first_row)
    curvature = contract_rows(lax.all_gather(scaled, "mp", axis=0, tiled=True), whole)
    return 2.0 * direction.astype(jnp.float32) - STEP * (curvature / whole.shape[0])


RING = (0, 2, 4, 6, 7, 5, 3, 1)
COUNT = len(RING)
UP = [(RING[i], RING[(i + 1) % COUNT]) for i in range(COUNT)]
DOWN = [(RING[i], RING[(i - 1) % COUNT]) for i in range(COUNT)]
CORE = [(i, i ^ 1) for i in range(4)]
ROW = [(i, i ^ 2) for i in range(4)]


def order_of(dp):
    at = RING.index(dp)
    seq = [(0, 0), (0, 1)]
    for k in range(1, COUNT // 2):
        seq += [(-k, 0), (-k, 1), (k, 0), (k, 1)]
    seq += [(COUNT // 2, 0), (COUNT // 2, 1)]
    return [2 * RING[(at + k) % COUNT] + h for k, h in seq]


ORDER = [order_of(d) for d in range(COUNT)]


WEIGHT = 0.15


def cost(flops):
    return pl.CostEstimate(flops=int(WEIGHT * flops), bytes_accessed=0, transcendentals=0)


IN_VMEM = pl.BlockSpec(memory_space=pltpu.VMEM)


KEEP, GIVE = (0, (0, 1)), (1, (0, 1))


def project_kernel(wanted, count, which_ref, w_ref, d_ref, *refs):
    parts, outs = refs[:count], refs[count : count + len(wanted)]
    part = w_ref.shape[0] // 2
    block, row = refs[-1] if count > 1 else parts[0], 0
    for ref in parts if count > 1 else ():
        block[row : row + ref.shape[0], :] = ref[...]
        row += ref.shape[0]
    for (flip, sources), out in zip(wanted, outs):
        which = which_ref[0] if flip == 0 else 1 - which_ref[0]
        rows = pl.ds(pl.multiple_of(which * part, part), part)
        for at, source in enumerate(sources):
            values = project_rows((w_ref, d_ref)[source][rows, :], block[...])
            out[at * part : (at + 1) * part, :] = values.astype(out.dtype)


def project(core, w_out, direction, parts, wanted):
    count = sum(v.shape[0] for v in parts)
    width, depth = w_out.shape
    return pl.pallas_call(
        functools.partial(project_kernel, wanted, len(parts)),
        out_shape=[jax.ShapeDtypeStruct((width // 2 * len(sources), count), jnp.bfloat16) for _, sources in wanted]
        + [jax.ShapeDtypeStruct((count, depth), jnp.bfloat16)] * (len(parts) > 1),
        in_specs=[pl.BlockSpec(memory_space=pltpu.SMEM)] + [IN_VMEM] * (2 + len(parts)),
        out_specs=[IN_VMEM] * (len(wanted) + (len(parts) > 1)),
        compiler_params=pltpu.CompilerParams(vmem_limit_bytes=20 * 2**20),
        cost_estimate=cost(sum(len(sources) for _, sources in wanted) * width * max(count, 256) * depth),
        name="project",
    )(core, w_out, direction, *parts)


def merge_kernel(kept_ref, *refs):
    *pieces, chip, sent = refs
    row = 0
    for piece in pieces:
        rows = slice(row, row + piece.shape[0])
        total = kept_ref[rows, :].astype(jnp.float32) + piece[...].astype(jnp.float32)
        chip[rows, :] = total
        sent[rows, :] = total.astype(sent.dtype)
        row += piece.shape[0]


def merge(kept, *pieces):
    return pl.pallas_call(
        merge_kernel,
        out_shape=[jax.ShapeDtypeStruct(kept.shape, jnp.float32), jax.ShapeDtypeStruct(kept.shape, jnp.bfloat16)],
        in_specs=[IN_VMEM] * (1 + len(pieces)),
        out_specs=[IN_VMEM] * 2,
        compiler_params=pltpu.CompilerParams(vmem_limit_bytes=6 * 2**20),
        cost_estimate=cost(0),
        name="merge",
    )(kept, *pieces)


def contract_kernel(count, step, tile, flips, last, which_ref, base_ref, *refs):
    size = len(flips) + 1
    terms, refs = [refs[size * i : size * i + size] for i in range(count)], refs[size * count :]
    width, depth = base_ref.shape
    part = width // 2
    tiles = depth // tile
    if last:
        *_, out, buffer, sem = refs
    else:
        (out,) = refs

    def rows_of(flip):
        which = which_ref[0] if flip == 0 else 1 - which_ref[0]
        return pl.ds(pl.multiple_of(which * part, part), part)

    def copy_of(i, flip):
        columns = slice(i * tile, (i + 1) * tile)
        return pltpu.make_async_copy(buffer.at[i], out.at[rows_of(flip), columns], sem.at[i])

    for i in range(tiles):
        columns = slice(i * tile, (i + 1) * tile)
        for at, flip in enumerate(flips):
            rows = rows_of(flip)
            total = sum(
                jnp.dot(term[at][...], term[-1][:, columns], preferred_element_type=jnp.float32) for term in terms
            )
            base = base_ref[rows, columns]
            if base.dtype == jnp.bfloat16:
                base = 2.0 * base.astype(jnp.float32)
            if last:
                buffer[i, :, :] = base - step * total
            else:
                out[rows, columns] = base - step * total
        if last:
            copy_of(i, flips[0]).start()
    if last:
        for i in range(tiles):
            copy_of(i, flips[0]).wait()


def contract(core, base, terms, step, flips=(0, 1), last=False, into=None):
    width, depth = base.shape
    tile = 512
    while depth % tile:
        tile //= 2
    tiles = depth // tile
    operands = [v for term in terms for v in term]
    held = [] if into is None else [into]
    return pl.pallas_call(
        functools.partial(contract_kernel, len(terms), step, tile, flips, last),
        out_shape=jax.ShapeDtypeStruct((width, depth), jnp.float32),
        in_specs=[pl.BlockSpec(memory_space=pltpu.SMEM)] + [IN_VMEM] * (1 + len(operands)) + [pl.BlockSpec(memory_space=pl.ANY)] * len(held),
        out_specs=pl.BlockSpec(memory_space=pl.ANY) if last else IN_VMEM,
        scratch_shapes=[pltpu.VMEM((tiles, width // 2, tile), jnp.float32), pltpu.SemaphoreType.DMA((tiles,))] if last else [],
        input_output_aliases={2 + len(operands): 0} if held else {},
        compiler_params=pltpu.CompilerParams(vmem_limit_bytes=20 * 2**20),
        cost_estimate=cost(2 * width * depth * sum(term[-1].shape[0] for term in terms)),
        name="contract",
    )(core, base, *operands, *held)


def on_device(hidden, w_out, direction, targets, codes, code_weights):
    dp = lax.axis_index("dp")
    mp = lax.axis_index("mp")
    core = mp % 2
    rows, width = hidden.shape[0], w_out.shape[0]
    half, part = rows // 2, width // 2
    tokens_all = rows * COUNT

    def swap(value, pairs):
        return lax.ppermute(value, "mp", pairs)

    def gate(*values):
        return lax.optimization_barrier(values)

    def step(pair):
        return lax.ppermute(pair[0], "dp", UP), lax.ppermute(pair[1], "dp", DOWN)

    def cols(value, which):
        return lax.dynamic_slice_in_dim(value, which * part, part, 1)

    two = jnp.concatenate([cols(targets, core), swap(cols(targets, 1 - core), CORE)], axis=0)
    other = swap(two, ROW)
    base = jnp.asarray(ORDER, jnp.int32)[dp] * half
    token = (base[:, None] + jnp.arange(half, dtype=jnp.int32)[None, :]).reshape(1, tokens_all)
    image, patch = token // PATCHES, token % PATCHES

    def look_up(table, index):
        at = jnp.arange(table.shape[0], dtype=jnp.int32)[:, None]
        return jnp.sum(jnp.where(index == at, table[:, None], 0), axis=0, keepdims=True)

    code = look_up(codes, image)
    weight = look_up(code_weights, code)
    row, col = patch // GRID, patch % GRID
    col = jnp.where(code % 2 == 1, GRID - 1 - col, col)
    row = jnp.where(code // 2 == 1, GRID - 1 - row, row)
    source = (image ^ mp) * PATCHES + row * GRID + col
    one_hot = (jnp.arange(tokens_all, dtype=jnp.int32)[:, None] == source).astype(jnp.bfloat16)

    one = core[None]

    def align(other):
        return contract_rows(jnp.concatenate([two, other], axis=0), one_hot)

    def add(kept, theirs):
        return kept.astype(jnp.float32) + theirs.astype(jnp.float32)

    def over_rows(chip):
        return swap(chip.astype(jnp.bfloat16), ROW)

    def weigh(aligned, chip, across, start):
        sums = add(chip, across)
        at = slice(start, start + sums.shape[1])
        slope = 1.0 - jnp.tanh(sums[:part] - aligned[:, at]) ** 2
        mine = (weight[:, at] * slope * sums[part:]).astype(jnp.bfloat16)
        return mine, swap(mine, CORE)

    hop1 = step((hidden, hidden))
    theirs0, kept0 = project(one, w_out, direction, [hidden], (GIVE, KEEP))
    chip0 = add(kept0, swap(theirs0, CORE))
    across0 = over_rows(chip0)

    hop2 = step(hop1)
    theirs1, kept1, block1 = project(one, w_out, direction, hop1, (GIVE, KEEP))
    chip1 = add(kept1, swap(theirs1, CORE))
    across1 = over_rows(chip1)
    *hop2, kept1, chip0, across0, other = gate(*hop2, kept1, chip0, across0, other)
    aligned = align(other)
    hop3 = step(hop2)
    theirs2, kept2, block2 = project(one, w_out, direction, hop2, (GIVE, KEEP))
    chip2 = add(kept2, swap(theirs2, CORE))
    across2 = over_rows(chip2)
    scaled0 = weigh(aligned, chip0, across0, 0)
    *hop3, kept2, chip1, across1 = gate(*hop3, kept2, chip1, across1)
    hop4 = step((hop3[0][:half], hop3[1][half:]))
    *theirs3, block3 = project(one, w_out, direction, hop3, ((1, (0,)), (1, (1,))))
    theirs3 = [swap(v, CORE) for v in theirs3]
    (kept3,) = project(one, w_out, direction, [block3], (KEEP,))
    chip3, sent3 = merge(kept3, *theirs3)
    across3 = swap(sent3, ROW)
    *hop4, kept3, chip2, across2, chip1 = gate(*hop4, kept3, chip2, across2, chip1)
    scaled1 = weigh(aligned, chip1, across1, rows)
    theirs4, block4 = project(one, w_out, direction, hop4, (GIVE,))
    theirs4 = swap(theirs4, CORE)
    (kept4,) = project(one, w_out, direction, [block4], (KEEP,))
    chip4 = add(kept4, theirs4)
    across4 = over_rows(chip4)
    share = STEP / tokens_all
    scaled2 = weigh(aligned, chip2, across2, 3 * rows)
    block2, chip4 = gate(block2, chip4)
    total = contract(one, direction, [(*scaled0, hidden), (*scaled1, block1), (*scaled2, block2)], share)
    total, chip3 = gate(total, chip3)
    scaled3 = weigh(aligned, chip3, across3, 5 * rows)
    mine3, chip4 = gate(scaled3[0], chip4)
    scaled4 = weigh(aligned, chip4, across4, 7 * rows)
    result = contract(one, total, [(mine3, block3), (scaled4[0], block4)], share, (0,), True)
    terms = [(scaled3[1], block3), (scaled4[1], block4)]
    return contract(one, total, terms, share, (1,), True, result)


def solution(mesh):
    planned = mesh.shape["dp"] == COUNT and mesh.shape["mp"] == 4
    return jax.shard_map(
        on_device if planned else on_device_any,
        mesh=mesh,
        in_specs=(P("dp", "mp"), P("dp", "mp"), P("dp", "mp"), P("mp", "dp"), P(), P()),
        out_specs=P("dp", "mp"),
        check_vma=False,
    )
```

```python
import functools

import jax
import jax.numpy as jnp
from jax import lax
from jax.experimental import pallas as pl
from jax.experimental.pallas import tpu as pltpu
from jax.sharding import PartitionSpec as P

GRID = 16
PATCHES = 256


STEP = 0.5


def contract_rows(left, right):
    return lax.dot_general(
        left, right, (((0,), (0,)), ((), ())), preferred_element_type=jnp.float32
    )


def weigh_rows(sums, targets, codes, code_weights, first_row):
    row_count = targets.shape[0]
    width = targets.shape[1]
    image_count = row_count // PATCHES
    image_codes = lax.dynamic_slice_in_dim(codes, first_row // PATCHES, image_count, 0)
    patch_grid = targets.reshape(image_count, GRID, GRID, width)
    horizontal = (image_codes % 2 == 1)[:, None, None, None]
    vertical = (image_codes // 2 == 1)[:, None, None, None]
    patch_grid = jnp.where(horizontal, patch_grid[:, :, ::-1], patch_grid)
    patch_grid = jnp.where(vertical, patch_grid[:, ::-1], patch_grid)
    aligned = patch_grid.reshape(row_count, width).astype(jnp.float32)
    outputs = sums[:, :width]
    moved = sums[:, width:]
    slope = 1.0 - jnp.tanh(outputs - aligned) ** 2
    image_weight = jnp.sum(
        jnp.where(
            image_codes[:, None] == jnp.arange(code_weights.shape[0], dtype=jnp.int32)[None, :],
            code_weights[None, :],
            0.0,
        ),
        axis=1,
    )
    product = (slope * moved).reshape(image_count, PATCHES, width) * image_weight[:, None, None]
    return product.reshape(row_count, width).astype(jnp.bfloat16)


def project_rows(rows_here, stacked):
    return lax.dot_general(
        rows_here, stacked, (((1,), (1,)), ((), ())), preferred_element_type=jnp.float32
    )


def on_device_any(hidden, w_out, direction, targets, codes, code_weights):
    stacked = jnp.concatenate([w_out, direction], axis=0)
    whole = lax.all_gather(hidden, "dp", axis=0, tiled=True)
    sums = lax.psum_scatter(
        project_rows(whole, stacked).astype(jnp.bfloat16), "mp", scatter_dimension=0, tiled=True
    ).astype(jnp.float32)
    first_row = lax.axis_index("mp") * targets.shape[0]
    scaled = weigh_rows(sums, targets, codes, code_weights, first_row)
    curvature = contract_rows(lax.all_gather(scaled, "mp", axis=0, tiled=True), whole)
    return 2.0 * direction.astype(jnp.float32) - STEP * (curvature / whole.shape[0])


RING = (0, 2, 4, 6, 7, 5, 3, 1)
COUNT = len(RING)
UP = [(RING[i], RING[(i + 1) % COUNT]) for i in range(COUNT)]
DOWN = [(RING[i], RING[(i - 1) % COUNT]) for i in range(COUNT)]
CORE = [(i, i ^ 1) for i in range(4)]
ROW = [(i, i ^ 2) for i in range(4)]


def order_of(dp):
    at = RING.index(dp)
    seq = [(0, 0), (0, 1)]
    for k in range(1, COUNT // 2):
        seq += [(-k, 0), (-k, 1), (k, 0), (k, 1)]
    seq += [(COUNT // 2, 0), (COUNT // 2, 1)]
    return [2 * RING[(at + k) % COUNT] + h for k, h in seq]


ORDER = [order_of(d) for d in range(COUNT)]


WEIGHT = 0.15


def cost(flops):
    return pl.CostEstimate(flops=int(WEIGHT * flops), bytes_accessed=0, transcendentals=0)


IN_VMEM = pl.BlockSpec(memory_space=pltpu.VMEM)


KEEP, GIVE = (0, (0, 1)), (1, (0, 1))


def project_kernel(wanted, count, which_ref, w_ref, d_ref, *refs):
    parts, outs = refs[:count], refs[count : count + len(wanted)]
    part = w_ref.shape[0] // 2
    block, row = refs[-1] if count > 1 else parts[0], 0
    for ref in parts if count > 1 else ():
        block[row : row + ref.shape[0], :] = ref[...]
        row += ref.shape[0]
    for (flip, sources), out in zip(wanted, outs):
        which = which_ref[0] if flip == 0 else 1 - which_ref[0]
        rows = pl.ds(pl.multiple_of(which * part, part), part)
        for at, source in enumerate(sources):
            values = project_rows((w_ref, d_ref)[source][rows, :], block[...])
            out[at * part : (at + 1) * part, :] = values.astype(out.dtype)


def project(core, w_out, direction, parts, wanted):
    count = sum(v.shape[0] for v in parts)
    width, depth = w_out.shape
    return pl.pallas_call(
        functools.partial(project_kernel, wanted, len(parts)),
        out_shape=[jax.ShapeDtypeStruct((width // 2 * len(sources), count), jnp.bfloat16) for _, sources in wanted]
        + [jax.ShapeDtypeStruct((count, depth), jnp.bfloat16)] * (len(parts) > 1),
        in_specs=[pl.BlockSpec(memory_space=pltpu.SMEM)] + [IN_VMEM] * (2 + len(parts)),
        out_specs=[IN_VMEM] * (len(wanted) + (len(parts) > 1)),
        compiler_params=pltpu.CompilerParams(vmem_limit_bytes=20 * 2**20),
        cost_estimate=cost(sum(len(sources) for _, sources in wanted) * width * max(count, 256) * depth),
        name="project",
    )(core, w_out, direction, *parts)


def merge_kernel(kept_ref, *refs):
    *pieces, chip, sent = refs
    row = 0
    for piece in pieces:
        rows = slice(row, row + piece.shape[0])
        total = kept_ref[rows, :].astype(jnp.float32) + piece[...].astype(jnp.float32)
        chip[rows, :] = total
        sent[rows, :] = total.astype(sent.dtype)
        row += piece.shape[0]


def merge(kept, *pieces):
    return pl.pallas_call(
        merge_kernel,
        out_shape=[jax.ShapeDtypeStruct(kept.shape, jnp.float32), jax.ShapeDtypeStruct(kept.shape, jnp.bfloat16)],
        in_specs=[IN_VMEM] * (1 + len(pieces)),
        out_specs=[IN_VMEM] * 2,
        compiler_params=pltpu.CompilerParams(vmem_limit_bytes=6 * 2**20),
        cost_estimate=cost(0),
        name="merge",
    )(kept, *pieces)


def contract_kernel(count, step, tile, flips, last, which_ref, base_ref, *refs):
    size = len(flips) + 1
    terms, refs = [refs[size * i : size * i + size] for i in range(count)], refs[size * count :]
    width, depth = base_ref.shape
    part = width // 2
    tiles = depth // tile
    if last:
        *_, out, buffer, sem = refs
    else:
        (out,) = refs

    def rows_of(flip):
        which = which_ref[0] if flip == 0 else 1 - which_ref[0]
        return pl.ds(pl.multiple_of(which * part, part), part)

    def copy_of(i, flip):
        columns = slice(i * tile, (i + 1) * tile)
        return pltpu.make_async_copy(buffer.at[i], out.at[rows_of(flip), columns], sem.at[i])

    for i in range(tiles):
        columns = slice(i * tile, (i + 1) * tile)
        for at, flip in enumerate(flips):
            rows = rows_of(flip)
            total = sum(
                jnp.dot(term[at][...], term[-1][:, columns], preferred_element_type=jnp.float32) for term in terms
            )
            base = base_ref[rows, columns]
            if base.dtype == jnp.bfloat16:
                base = 2.0 * base.astype(jnp.float32)
            if last:
                buffer[i, :, :] = base - step * total
            else:
                out[rows, columns] = base - step * total
        if last:
            copy_of(i, flips[0]).start()
    if last:
        for i in range(tiles):
            copy_of(i, flips[0]).wait()


def contract(core, base, terms, step, flips=(0, 1), last=False, into=None):
    width, depth = base.shape
    tile = 512
    while depth % tile:
        tile //= 2
    tiles = depth // tile
    operands = [v for term in terms for v in term]
    held = [] if into is None else [into]
    return pl.pallas_call(
        functools.partial(contract_kernel, len(terms), step, tile, flips, last),
        out_shape=jax.ShapeDtypeStruct((width, depth), jnp.float32),
        in_specs=[pl.BlockSpec(memory_space=pltpu.SMEM)] + [IN_VMEM] * (1 + len(operands)) + [pl.BlockSpec(memory_space=pl.ANY)] * len(held),
        out_specs=pl.BlockSpec(memory_space=pl.ANY) if last else IN_VMEM,
        scratch_shapes=[pltpu.VMEM((tiles, width // 2, tile), jnp.float32), pltpu.SemaphoreType.DMA((tiles,))] if last else [],
        input_output_aliases={2 + len(operands): 0} if held else {1: 0} if not last and len(flips) == 1 else {},
        compiler_params=pltpu.CompilerParams(vmem_limit_bytes=20 * 2**20),
        cost_estimate=cost(2 * width * depth * sum(term[-1].shape[0] for term in terms)),
        name="contract",
    )(core, base, *operands, *held)


def on_device(hidden, w_out, direction, targets, codes, code_weights):
    dp = lax.axis_index("dp")
    mp = lax.axis_index("mp")
    core = mp % 2
    rows, width = hidden.shape[0], w_out.shape[0]
    half, part = rows // 2, width // 2
    tokens_all = rows * COUNT

    def swap(value, pairs):
        return lax.ppermute(value, "mp", pairs)

    def gate(*values):
        return lax.optimization_barrier(values)

    def step(pair):
        return lax.ppermute(pair[0], "dp", UP), lax.ppermute(pair[1], "dp", DOWN)

    def cols(value, which):
        return lax.dynamic_slice_in_dim(value, which * part, part, 1)

    two = jnp.concatenate([cols(targets, core), swap(cols(targets, 1 - core), CORE)], axis=0)
    other = swap(two, ROW)
    base = jnp.asarray(ORDER, jnp.int32)[dp] * half
    token = (base[:, None] + jnp.arange(half, dtype=jnp.int32)[None, :]).reshape(1, tokens_all)
    image, patch = token // PATCHES, token % PATCHES

    def look_up(table, index):
        at = jnp.arange(table.shape[0], dtype=jnp.int32)[:, None]
        return jnp.sum(jnp.where(index == at, table[:, None], 0), axis=0, keepdims=True)

    code = look_up(codes, image)
    weight = look_up(code_weights, code)
    row, col = patch // GRID, patch % GRID
    col = jnp.where(code % 2 == 1, GRID - 1 - col, col)
    row = jnp.where(code // 2 == 1, GRID - 1 - row, row)
    source = (image ^ mp) * PATCHES + row * GRID + col
    one_hot = (jnp.arange(tokens_all, dtype=jnp.int32)[:, None] == source).astype(jnp.bfloat16)

    one = core[None]

    def align(other):
        return contract_rows(jnp.concatenate([two, other], axis=0), one_hot)

    def add(kept, theirs):
        return kept.astype(jnp.float32) + theirs.astype(jnp.float32)

    def over_rows(chip):
        return swap(chip.astype(jnp.bfloat16), ROW)

    def weigh(aligned, chip, across, start):
        sums = add(chip, across)
        at = slice(start, start + sums.shape[1])
        slope = 1.0 - jnp.tanh(sums[:part] - aligned[:, at]) ** 2
        mine = (weight[:, at] * slope * sums[part:]).astype(jnp.bfloat16)
        return mine, swap(mine, CORE)

    hop1 = step((hidden, hidden))
    theirs0, kept0 = project(one, w_out, direction, [hidden], (GIVE, KEEP))
    chip0 = add(kept0, swap(theirs0, CORE))
    across0 = over_rows(chip0)

    hop2 = step(hop1)
    theirs1, kept1, block1 = project(one, w_out, direction, hop1, (GIVE, KEEP))
    chip1 = add(kept1, swap(theirs1, CORE))
    across1 = over_rows(chip1)
    *hop2, kept1, chip0, across0, other = gate(*hop2, kept1, chip0, across0, other)
    aligned = align(other)
    hop3 = step(hop2)
    theirs2, kept2, block2 = project(one, w_out, direction, hop2, (GIVE, KEEP))
    chip2 = add(kept2, swap(theirs2, CORE))
    across2 = over_rows(chip2)
    scaled0 = weigh(aligned, chip0, across0, 0)
    *hop3, kept2, chip1, across1 = gate(*hop3, kept2, chip1, across1)
    hop4 = step((hop3[0][:half], hop3[1][half:]))
    *theirs3, block3 = project(one, w_out, direction, hop3, ((1, (0,)), (1, (1,))))
    theirs3 = [swap(v, CORE) for v in theirs3]
    (kept3,) = project(one, w_out, direction, [block3], (KEEP,))
    chip3, sent3 = merge(kept3, *theirs3)
    across3 = swap(sent3, ROW)
    *hop4, kept3, chip2, across2, chip1 = gate(*hop4, kept3, chip2, across2, chip1)
    scaled1 = weigh(aligned, chip1, across1, rows)
    theirs4, block4 = project(one, w_out, direction, hop4, (GIVE,))
    theirs4 = swap(theirs4, CORE)
    (kept4,) = project(one, w_out, direction, [block4], (KEEP,))
    chip4 = add(kept4, theirs4)
    across4 = over_rows(chip4)
    share = STEP / tokens_all
    scaled2 = weigh(aligned, chip2, across2, 3 * rows)
    block2, chip4 = gate(block2, chip4)
    total = contract(one, direction, [(*scaled0, hidden), (*scaled1, block1), (*scaled2, block2)], share)
    total, chip3 = gate(total, chip3)
    scaled3 = weigh(aligned, chip3, across3, 5 * rows)
    total = contract(one, total, [(scaled3[0], block3)], share, (0,))
    total, chip4 = gate(total, chip4)
    scaled4 = weigh(aligned, chip4, across4, 7 * rows)
    result = contract(one, total, [(scaled4[0], block4)], share, (0,), True)
    terms = [(scaled3[1], block3), (scaled4[1], block4)]
    return contract(one, total, terms, share, (1,), True, result)


def solution(mesh):
    planned = mesh.shape["dp"] == COUNT and mesh.shape["mp"] == 4
    return jax.shard_map(
        on_device if planned else on_device_any,
        mesh=mesh,
        in_specs=(P("dp", "mp"), P("dp", "mp"), P("dp", "mp"), P("mp", "dp"), P(), P()),
        out_specs=P("dp", "mp"),
        check_vma=False,
    )
```

```python
import functools

import jax
import jax.numpy as jnp
from jax import lax
from jax.experimental import pallas as pl
from jax.experimental.pallas import tpu as pltpu
from jax.sharding import PartitionSpec as P

GRID = 16
PATCHES = 256


STEP = 0.5


def contract_rows(left, right):
    return lax.dot_general(
        left, right, (((0,), (0,)), ((), ())), preferred_element_type=jnp.float32
    )


def weigh_rows(sums, targets, codes, code_weights, first_row):
    row_count = targets.shape[0]
    width = targets.shape[1]
    image_count = row_count // PATCHES
    image_codes = lax.dynamic_slice_in_dim(codes, first_row // PATCHES, image_count, 0)
    patch_grid = targets.reshape(image_count, GRID, GRID, width)
    horizontal = (image_codes % 2 == 1)[:, None, None, None]
    vertical = (image_codes // 2 == 1)[:, None, None, None]
    patch_grid = jnp.where(horizontal, patch_grid[:, :, ::-1], patch_grid)
    patch_grid = jnp.where(vertical, patch_grid[:, ::-1], patch_grid)
    aligned = patch_grid.reshape(row_count, width).astype(jnp.float32)
    outputs = sums[:, :width]
    moved = sums[:, width:]
    slope = 1.0 - jnp.tanh(outputs - aligned) ** 2
    image_weight = jnp.sum(
        jnp.where(
            image_codes[:, None] == jnp.arange(code_weights.shape[0], dtype=jnp.int32)[None, :],
            code_weights[None, :],
            0.0,
        ),
        axis=1,
    )
    product = (slope * moved).reshape(image_count, PATCHES, width) * image_weight[:, None, None]
    return product.reshape(row_count, width).astype(jnp.bfloat16)


def project_rows(rows_here, stacked):
    return lax.dot_general(
        rows_here, stacked, (((1,), (1,)), ((), ())), preferred_element_type=jnp.float32
    )


def on_device_any(hidden, w_out, direction, targets, codes, code_weights):
    stacked = jnp.concatenate([w_out, direction], axis=0)
    whole = lax.all_gather(hidden, "dp", axis=0, tiled=True)
    sums = lax.psum_scatter(
        project_rows(whole, stacked).astype(jnp.bfloat16), "mp", scatter_dimension=0, tiled=True
    ).astype(jnp.float32)
    first_row = lax.axis_index("mp") * targets.shape[0]
    scaled = weigh_rows(sums, targets, codes, code_weights, first_row)
    curvature = contract_rows(lax.all_gather(scaled, "mp", axis=0, tiled=True), whole)
    return 2.0 * direction.astype(jnp.float32) - STEP * (curvature / whole.shape[0])


RING = (0, 2, 4, 6, 7, 5, 3, 1)
COUNT = len(RING)
UP = [(RING[i], RING[(i + 1) % COUNT]) for i in range(COUNT)]
DOWN = [(RING[i], RING[(i - 1) % COUNT]) for i in range(COUNT)]
CORE = [(i, i ^ 1) for i in range(4)]
ROW = [(i, i ^ 2) for i in range(4)]


def order_of(dp):
    at = RING.index(dp)
    seq = [(0, 0), (0, 1)]
    for k in range(1, COUNT // 2):
        seq += [(-k, 0), (-k, 1), (k, 0), (k, 1)]
    seq += [(COUNT // 2, 0), (COUNT // 2, 1)]
    return [2 * RING[(at + k) % COUNT] + h for k, h in seq]


ORDER = [order_of(d) for d in range(COUNT)]


WEIGHT = 0.15


def cost(flops):
    return pl.CostEstimate(flops=int(WEIGHT * flops), bytes_accessed=0, transcendentals=0)


IN_VMEM = pl.BlockSpec(memory_space=pltpu.VMEM)


KEEP, GIVE = (0, (0, 1)), (1, (0, 1))


def project_kernel(wanted, count, which_ref, w_ref, d_ref, *refs):
    parts, outs = refs[:count], refs[count : count + len(wanted)]
    part = w_ref.shape[0] // 2
    block, row = refs[-1] if count > 1 else parts[0], 0
    for ref in parts if count > 1 else ():
        block[row : row + ref.shape[0], :] = ref[...]
        row += ref.shape[0]
    for (flip, sources), out in zip(wanted, outs):
        which = which_ref[0] if flip == 0 else 1 - which_ref[0]
        rows = pl.ds(pl.multiple_of(which * part, part), part)
        for at, source in enumerate(sources):
            values = project_rows((w_ref, d_ref)[source][rows, :], block[...])
            out[at * part : (at + 1) * part, :] = values.astype(out.dtype)


def project(core, w_out, direction, parts, wanted):
    count = sum(v.shape[0] for v in parts)
    width, depth = w_out.shape
    return pl.pallas_call(
        functools.partial(project_kernel, wanted, len(parts)),
        out_shape=[jax.ShapeDtypeStruct((width // 2 * len(sources), count), jnp.bfloat16) for _, sources in wanted]
        + [jax.ShapeDtypeStruct((count, depth), jnp.bfloat16)] * (len(parts) > 1),
        in_specs=[pl.BlockSpec(memory_space=pltpu.SMEM)] + [IN_VMEM] * (2 + len(parts)),
        out_specs=[IN_VMEM] * (len(wanted) + (len(parts) > 1)),
        compiler_params=pltpu.CompilerParams(vmem_limit_bytes=20 * 2**20),
        cost_estimate=cost(sum(len(sources) for _, sources in wanted) * width * max(count, 256) * depth),
        name="project",
    )(core, w_out, direction, *parts)


def merge_kernel(kept_ref, *refs):
    *pieces, chip, sent = refs
    row = 0
    for piece in pieces:
        rows = slice(row, row + piece.shape[0])
        total = kept_ref[rows, :].astype(jnp.float32) + piece[...].astype(jnp.float32)
        chip[rows, :] = total
        sent[rows, :] = total.astype(sent.dtype)
        row += piece.shape[0]


def merge(kept, *pieces):
    return pl.pallas_call(
        merge_kernel,
        out_shape=[jax.ShapeDtypeStruct(kept.shape, jnp.float32), jax.ShapeDtypeStruct(kept.shape, jnp.bfloat16)],
        in_specs=[IN_VMEM] * (1 + len(pieces)),
        out_specs=[IN_VMEM] * 2,
        compiler_params=pltpu.CompilerParams(vmem_limit_bytes=6 * 2**20),
        cost_estimate=cost(0),
        name="merge",
    )(kept, *pieces)


def contract_kernel(count, step, tile, flips, last, which_ref, base_ref, *refs):
    size = len(flips) + 1
    terms, refs = [refs[size * i : size * i + size] for i in range(count)], refs[size * count :]
    width, depth = base_ref.shape
    part = width // 2
    tiles = depth // tile
    if last:
        *_, out, buffer, sem = refs
    else:
        (out,) = refs

    def rows_of(flip):
        which = which_ref[0] if flip == 0 else 1 - which_ref[0]
        return pl.ds(pl.multiple_of(which * part, part), part)

    def copy_of(i, flip):
        columns = slice(i * tile, (i + 1) * tile)
        return pltpu.make_async_copy(buffer.at[i], out.at[rows_of(flip), columns], sem.at[i])

    for i in range(tiles):
        columns = slice(i * tile, (i + 1) * tile)
        for at, flip in enumerate(flips):
            rows = rows_of(flip)
            total = sum(
                jnp.dot(term[at][...], term[-1][:, columns], preferred_element_type=jnp.float32) for term in terms
            )
            base = base_ref[rows, columns]
            if base.dtype == jnp.bfloat16:
                base = 2.0 * base.astype(jnp.float32)
            if last:
                buffer[i, :, :] = base - step * total
            else:
                out[rows, columns] = base - step * total
        if last:
            copy_of(i, flips[0]).start()
    if last:
        for i in range(tiles):
            copy_of(i, flips[0]).wait()


def contract(core, base, terms, step, flips=(0, 1), last=False, into=None):
    width, depth = base.shape
    tile = 512
    while depth % tile:
        tile //= 2
    tiles = depth // tile
    operands = [v for term in terms for v in term]
    held = [] if into is None else [into]
    return pl.pallas_call(
        functools.partial(contract_kernel, len(terms), step, tile, flips, last),
        out_shape=jax.ShapeDtypeStruct((width, depth), jnp.float32),
        in_specs=[pl.BlockSpec(memory_space=pltpu.SMEM)] + [IN_VMEM] * (1 + len(operands)) + [pl.BlockSpec(memory_space=pl.ANY)] * len(held),
        out_specs=pl.BlockSpec(memory_space=pl.ANY) if last else IN_VMEM,
        scratch_shapes=[pltpu.VMEM((tiles, width // 2, tile), jnp.float32), pltpu.SemaphoreType.DMA((tiles,))] if last else [],
        input_output_aliases={2 + len(operands): 0} if held else {1: 0} if not last and len(flips) == 1 else {},
        compiler_params=pltpu.CompilerParams(vmem_limit_bytes=20 * 2**20),
        cost_estimate=cost(2 * width * depth * sum(term[-1].shape[0] for term in terms)),
        name="contract",
    )(core, base, *operands, *held)


def on_device(hidden, w_out, direction, targets, codes, code_weights):
    dp = lax.axis_index("dp")
    mp = lax.axis_index("mp")
    core = mp % 2
    rows, width = hidden.shape[0], w_out.shape[0]
    half, part = rows // 2, width // 2
    tokens_all = rows * COUNT

    def swap(value, pairs):
        return lax.ppermute(value, "mp", pairs)

    def gate(*values):
        return lax.optimization_barrier(values)

    def step(pair):
        return lax.ppermute(pair[0], "dp", UP), lax.ppermute(pair[1], "dp", DOWN)

    def cols(value, which):
        return lax.dynamic_slice_in_dim(value, which * part, part, 1)

    two = jnp.concatenate([cols(targets, core), swap(cols(targets, 1 - core), CORE)], axis=0)
    other = swap(two, ROW)
    base = jnp.asarray(ORDER, jnp.int32)[dp] * half
    token = (base[:, None] + jnp.arange(half, dtype=jnp.int32)[None, :]).reshape(1, tokens_all)
    image, patch = token // PATCHES, token % PATCHES

    def look_up(table, index):
        at = jnp.arange(table.shape[0], dtype=jnp.int32)[:, None]
        return jnp.sum(jnp.where(index == at, table[:, None], 0), axis=0, keepdims=True)

    code = look_up(codes, image)
    weight = look_up(code_weights, code)
    row, col = patch // GRID, patch % GRID
    col = jnp.where(code % 2 == 1, GRID - 1 - col, col)
    row = jnp.where(code // 2 == 1, GRID - 1 - row, row)
    source = (image ^ mp) * PATCHES + row * GRID + col
    one_hot = (jnp.arange(tokens_all, dtype=jnp.int32)[:, None] == source).astype(jnp.bfloat16)

    one = core[None]

    def align(other):
        return contract_rows(jnp.concatenate([two, other], axis=0), one_hot)

    def add(kept, theirs):
        return kept.astype(jnp.float32) + theirs.astype(jnp.float32)

    def over_rows(chip):
        return swap(chip.astype(jnp.bfloat16), ROW)

    def weigh(aligned, chip, across, start):
        sums = add(chip, across)
        at = slice(start, start + sums.shape[1])
        slope = 1.0 - jnp.tanh(sums[:part] - aligned[:, at]) ** 2
        mine = (weight[:, at] * slope * sums[part:]).astype(jnp.bfloat16)
        return mine, swap(mine, CORE)

    hop1 = step((hidden, hidden))
    theirs0, kept0 = project(one, w_out, direction, [hidden], (GIVE, KEEP))
    chip0 = add(kept0, swap(theirs0, CORE))
    across0 = over_rows(chip0)

    hop2 = step(hop1)
    theirs1, kept1, block1 = project(one, w_out, direction, hop1, (GIVE, KEEP))
    chip1 = add(kept1, swap(theirs1, CORE))
    across1 = over_rows(chip1)
    *hop2, kept1, chip0, across0, other = gate(*hop2, kept1, chip0, across0, other)
    aligned = align(other)
    hop3 = step(hop2)
    theirs2, kept2, block2 = project(one, w_out, direction, hop2, (GIVE, KEEP))
    chip2 = add(kept2, swap(theirs2, CORE))
    across2 = over_rows(chip2)
    scaled0 = weigh(aligned, chip0, across0, 0)
    hop4 = step((hop3[0][:half], hop3[1][half:]))
    *hop3, kept2, chip1, across1 = gate(*hop3, kept2, chip1, across1)
    *theirs3, block3 = project(one, w_out, direction, hop3, ((1, (0,)), (1, (1,))))
    theirs3 = [swap(v, CORE) for v in theirs3]
    (kept3,) = project(one, w_out, direction, [block3], (KEEP,))
    chip3, sent3 = merge(kept3, *theirs3)
    across3 = swap(sent3, ROW)
    *hop4, kept3, chip2, across2, chip1 = gate(*hop4, kept3, chip2, across2, chip1)
    scaled1 = weigh(aligned, chip1, across1, rows)
    theirs4, block4 = project(one, w_out, direction, hop4, (GIVE,))
    theirs4 = swap(theirs4, CORE)
    (kept4,) = project(one, w_out, direction, [block4], (KEEP,))
    chip4 = add(kept4, theirs4)
    across4 = over_rows(chip4)
    share = STEP / tokens_all
    scaled2 = weigh(aligned, chip2, across2, 3 * rows)
    block2, chip4 = gate(block2, chip4)
    total = contract(one, direction, [(*scaled0, hidden), (*scaled1, block1), (*scaled2, block2)], share)
    total, chip3 = gate(total, chip3)
    scaled3 = weigh(aligned, chip3, across3, 5 * rows)
    total = contract(one, total, [(scaled3[0], block3)], share, (0,))
    total, chip4 = gate(total, chip4)
    scaled4 = weigh(aligned, chip4, across4, 7 * rows)
    result = contract(one, total, [(scaled4[0], block4)], share, (0,), True)
    terms = [(scaled3[1], block3), (scaled4[1], block4)]
    return contract(one, total, terms, share, (1,), True, result)


def solution(mesh):
    planned = mesh.shape["dp"] == COUNT and mesh.shape["mp"] == 4
    return jax.shard_map(
        on_device if planned else on_device_any,
        mesh=mesh,
        in_specs=(P("dp", "mp"), P("dp", "mp"), P("dp", "mp"), P("mp", "dp"), P(), P()),
        out_specs=P("dp", "mp"),
        check_vma=False,
    )
```
